256 devices in a mesh: elec: 4 (over z_hi), cell: 32 (over y, x, z_lo), gate: 2 (over core).
Axes of the slice: x: 4, y: 4, z: 8 (z_hi: 4, z_lo: 2; z = z_hi * 2 + z_lo), core: 2. Of those that a mesh axis runs over, the one named last changes fastest.
Arguments:
- panels: bfloat16 [3, 2048, 8192], P(None, 'elec', 'cell'), may hold values from -6 to 6
- conductivity: float32 [8192], P('cell'), may hold values from 0.3 to 3
- residuals: bfloat16 [16, 16, 4, 128, 128], P('gate', 'elec', None, 'cell'), may hold values from -0.01171875 to 0.01171875
- gate_weight: float32 [16], P('gate'), may hold values from 0.3 to 2
- pattern: int32 [16, 4], P('elec'), may hold values from 0 to 15, as said below
- live_count: int32 [16], P('elec'), may hold values from 1 to 4, as said below
Outputs:
- grad: float32 [16, 8192], P('gate', 'cell')
- update: float32 [8192], P('cell')
The draws below stay inside these ranges and needn't reach their ends.
Inputs may be any that keep to these rules, and one draw needn't show every extreme that they name: `pattern`: the entries of a row are distinct block numbers, and the first entry of row i is i itself; every block number appears. `live_count`: both ends are reached in every draw.
All inputs are finite; a program needn't handle non-finite values.
Results may differ from the reference program's by a relative error of at most 0.0003.
Values may be sent and summed in bfloat16 or wider, within the bound.
A program may use at most 64 MiB of HBM per device.

```python
import math
import jax
import jax.numpy as jnp
from jax import lax

E = 2048
BLK = 128
TG = 16
KMAX = 4
NB = 16
CELLS = 8192


def draw_pattern(key, part):
    key = jax.random.fold_in(key, 11)
    keys = jax.random.split(key, NB)
    others = jax.vmap(lambda single: jax.random.permutation(single, NB - 1)[:KMAX - 1])(keys)
    own = jnp.arange(NB, dtype=jnp.int32)
    rest = (own[:, None] + 1 + others.astype(jnp.int32)) % NB
    return jnp.concatenate([own[:, None], rest], axis=1).astype(jnp.int32)


def draw_live_count(key, part):
    key = jax.random.fold_in(key, 23)
    first, second, third = jax.random.split(key, 3)
    counts = jax.random.randint(first, (NB,), 1, KMAX + 1)
    spot = jax.random.randint(second, (), 0, NB)
    other = (spot + 1 + jax.random.randint(third, (), 0, NB - 1)) % NB
    places = jnp.arange(NB)
    counts = jnp.where(places == spot, KMAX, counts)
    counts = jnp.where(places == other, 1, counts)
    return counts.astype(jnp.int32)


def block_scale(key, extent, cuts, smallest, largest):
    def one(axis_at, blocks):
        steps = jax.random.uniform(jax.random.fold_in(jax.random.fold_in(key, 6), axis_at), (blocks,), jnp.float32, smallest / len(cuts), largest / len(cuts))
        return jnp.repeat(jnp.exp(steps), extent[axis_at] // blocks).reshape((-1,) + (1,) * (len(extent) - axis_at - 1))

    loudness = one(*cuts[0])
    for cut in cuts[1:]:
        loudness = loudness * one(*cut)
    return loudness


def scatter_about(key, dims, scale, bound, shards=(), held_as=jnp.bfloat16):
    drawn = scale * jax.random.normal(key, dims, jnp.float32)
    if shards:
        drawn = drawn * block_scale(key, dims, shards, -0.22, 0.18)
    return jnp.clip(drawn, -bound, bound).astype(held_as)


def setup_inputs(seed: int = 0) -> dict:
    key_list = jax.random.split(jax.random.key(seed), 7)
    panels = scatter_about(key_list[0], (3, E, CELLS), 1.0, 6.0, ((1, 4), (2, 32)))
    conductivity = jnp.clip(jnp.exp(math.log(3.0) - 2.3025851 * jax.random.uniform(key_list[1], (CELLS,), jnp.float32) ** block_scale(key_list[1], (CELLS,), ((0, 32),), -0.2, 0.2)), 0.3, 3.0)
    residuals = scatter_about(key_list[2], (TG, NB, KMAX, BLK, BLK), (1.0 / (BLK * 4)), 0.01171875, ((0, 2), (1, 4), (3, 32)))
    gate_weight = jnp.clip(0.3 + 1.7 * jax.random.uniform(key_list[3], (TG,), jnp.float32) ** block_scale(key_list[3], (TG,), ((0, 2),), -0.2, 0.2), 0.3, 2.0)
    pattern = draw_pattern(jax.random.fold_in(key_list[6], 71), 0)
    live_count = draw_live_count(jax.random.fold_in(key_list[6], 71), 0)
    return dict(panels=panels, conductivity=conductivity, residuals=residuals, gate_weight=gate_weight, pattern=pattern, live_count=live_count)


def reference(panels, conductivity, residuals, gate_weight, pattern, live_count):
    def visit_pair(position, running):
        row_block = position // KMAX
        column = position % KMAX
        target_block = pattern[row_block, column]
        source = lax.dynamic_slice_in_dim(panels, (row_block * BLK).astype(jnp.int32), BLK, 1).astype(jnp.float32)
        target = lax.dynamic_slice_in_dim(panels, (target_block * BLK).astype(jnp.int32), BLK, 1).astype(jnp.float32)
        block = lax.dynamic_index_in_dim(lax.dynamic_index_in_dim(residuals, row_block, 1, False), column, 1, False).astype(jnp.float32)
        mixed = jnp.einsum("tab,mbc->tmac", block, target)
        term = jnp.einsum("tmac,mac->tc", mixed, source)
        weight = jnp.where(column < live_count[row_block], jnp.float32(1.0), jnp.float32(0.0))
        return running + weight * term

    start = jnp.zeros((TG, CELLS), jnp.float32)
    total = lax.fori_loop(0, NB * KMAX, visit_pair, start)
    grad = -conductivity[None, :] * total
    update = jnp.sum(gate_weight[:, None] * grad, axis=0)
    return grad, update
```

```python
import jax
import jax.numpy as jnp
from jax import lax
from jax.experimental import pallas as pl
from jax.experimental.pallas import tpu as pltpu
from jax.sharding import PartitionSpec as P

MESH = pl.DeviceIdType.MESH
NX, NY, NZ = 4, 4, 8
D1 = (0, 1, -1, 2)

ORDER = (
    "L10", "V0", "UA+", "UA-", "UB+0", "UB-0", "S10", "L11", "L12", "VA+", "VB+0", "VA-", "VB-0",
    "S11", "L20", "UA2+", "UA2-", "UB+1", "UB-1", "L21", "VB+1", "VB-1", "S12", "L22", "UB+-1",
    "UB--1", "VB+-1", "VB--1", "L30", "VA2+", "VA2-", "L31", "UB+2", "UB-2", "L32", "VB+2", "VB-2",
    "S20",
)


def kernel(
    p_hbm, r_ref, cond_ref, gw_ref, pat_ref, live_ref,
    grad_ref, upd_ref,
    rbuf, pall0, pall1, pall2, via, psf, mix, part, gath, rows, send, recv, local,
):
    pall = (pall0, pall1, pall2)
    cell = lax.axis_index("cell")
    e = lax.axis_index("elec")
    g = lax.axis_index("gate")
    y, x, zl = cell // (NX * 2), (cell // 2) % NX, cell % 2
    z = e * 2 + zl
    sg = 1 - 2 * g

    def cell_at(dx, dy, zlow):
        return (((y + dy + NY) % NY) * NX + (x + dx + NX) % NX) * 2 + zlow

    def xy(dx, dy):
        return {"cell": cell_at(dx, dy, zl), "elec": e, "gate": g}

    def at_z(dz, core=None):
        zz = (z + dz + 2 * NZ) % NZ
        return {"cell": cell_at(0, 0, zz % 2), "elec": zz // 2, "gate": g if core is None else core}

    z_mate = at_z(1 - 2 * zl)
    core_mate = {"cell": cell, "elec": e, "gate": 1 - g}
    peers = [at_z(d) for d in (2, 4, 6)]
    cross = [at_z(d, 1 - g) for d in (0, 2, 4, 6)]

    barrier = pltpu.get_barrier_semaphore()
    greet = [xy(1, 0), xy(-1, 0), xy(0, 1), xy(0, -1), at_z(1), at_z(-1)] + peers + cross
    for device in greet:
        pl.semaphore_signal(barrier, inc=1, device_id=device, device_id_type=MESH)

    own = [
        pltpu.make_async_copy(p_hbm.at[m], pall[m].at[pl.ds(e * 4, 4)], local.at[m])
        for m in range(3)
    ]
    for copy in own:
        copy.start()

    out_row = lax.broadcasted_iota(jnp.int32, (512, 512), 0)
    in_row = lax.broadcasted_iota(jnp.int32, (512, 512), 1)
    shuffle = jnp.where((out_row % 8) * 64 + out_row // 8 == in_row, 1.0, 0.0).astype(jnp.bfloat16)
    turned = jnp.dot(shuffle, r_ref[...], preferred_element_type=jnp.float32)
    rbuf[cell] = turned.astype(jnp.bfloat16).reshape(16, 32, 128)

    pl.semaphore_wait(barrier, len(greet))

    ids = {}
    flying = []
    landing = {}

    def go(name, src, dst, device):
        n = ids.setdefault(name, len(ids))
        copy = pltpu.make_async_remote_copy(
            src_ref=src, dst_ref=dst, send_sem=send.at[n], recv_sem=recv.at[n],
            device_id=device, device_id_type=MESH,
        )
        copy.start()
        flying.append(copy)
        landing[name] = copy

    def block(name, slot, half, device):
        ref = rbuf.at[slot] if half is None else rbuf.at[slot, pl.ds(half * 8, 8)]
        go(name, ref, ref, device)

    def step(s, axis, sign):
        along_x = (axis == 0) == (s == "U")
        return xy(sign, 0) if along_x else xy(0, sign)

    def slot_of(s, d1, d2):
        if s == "U":
            return cell_at(-d1, -d2, zl)
        return cell_at(-d2, -d1, 1 - zl)

    def panel(dz):
        origin = ((z + dz + 2 * NZ) % NZ) // 2
        return pl.ds(origin * 4 + g * 2, 2)

    def seed(s):
        slot = slot_of(s, 0, 0)
        for axis, tag, tail in ((0, "A", ""), (1, "B", "0")):
            for sign, mark in ((1, "+"), (-1, "-")):
                block(s + tag + mark + tail, slot, None, step(s, axis, sign))

    def spread(s, d1):
        slot = slot_of(s, d1, 0)
        for sign, mark in ((1, "+"), (-1, "-")):
            block(f"{s}B{mark}{d1}", slot, None, step(s, 1, sign))

    def arrived(name):
        landing[name].wait_recv()

    def pass_on(name):
        if name == "V0":
            seed("V")
        elif name[0] in "UV" and name[1:3] == "A2":
            s = name[0]
            if name[3] == "-":
                spread(s, 2)
        elif name[0] in "UV" and name[1] == "A":
            s, mark = name[0], name[2]
            sign = 1 if mark == "+" else -1
            block(f"{s}A2{mark}", slot_of(s, sign, 0), 0 if sign == 1 else 1, step(s, 0, sign))
            spread(s, sign)
        elif name[0] in "UV" and name[1:3] != "B2":
            s, mark, d1 = name[0], name[2], int(name[3:])
            sign = 1 if mark == "+" else -1
            block(f"{s}B2{mark}{d1}", slot_of(s, d1, sign), 0 if sign == 1 else 1, step(s, 1, sign))
        elif name[0] in "LS":
            m = int(name[2])
            kind = name[:2]
            if kind == "L1":
                go(f"L2{m}", via.at[0, m], pall[m].at[panel(-sg)], at_z(sg))
            elif kind == "L2":
                ref = pall[m].at[panel(-2 * sg)]
                go(f"L3{m}", ref, via.at[1, m], at_z(sg))
                go(f"W2{m}", ref, ref, core_mate)
            elif kind == "L3":
                go(f"L4{m}", via.at[1, m], pall[m].at[panel(-3 * sg)], at_z(sg))
            elif kind == "L4":
                ref = pall[m].at[panel(4)]
                go(f"W4{m}", ref, ref, core_mate)
            elif kind == "S1":
                go(f"S2{m}", via.at[2, m], pall[m].at[panel(sg)], at_z(-sg))
            elif kind == "S2":
                ref = pall[m].at[panel(2 * sg)]
                go(f"WS{m}", ref, ref, core_mate)

    block("V0", cell, None, z_mate)
    seed("U")
    half = pl.ds(g * 2, 2)
    for m in range(3):
        go(f"L1{m}", p_hbm.at[m, half], via.at[0, m], at_z(sg))
        go(f"S1{m}", p_hbm.at[m, half], via.at[2, m], at_z(-sg))

    for m in range(3):
        own[m].wait()
        psf[m] = pall[m][pl.ds(e * 4, 4)].reshape(512, 256).astype(jnp.float32)

    waited = set()

    def take(name):
        arrived(name)
        waited.add(name)
        pass_on(name)

    for name in ORDER:
        take(name)
    for name in list(ids):
        if name[0] in "UV" and name not in waited:
            take(name)

    def component(m, total):
        def source(i, acc):
            count = live_ref[i]
            target = []
            for k in range(4):
                there = pall[m][pat_ref[i, k]]
                alive = jnp.minimum(jnp.maximum(count - k, 0), 1).astype(jnp.float32)
                target.append(there * jnp.full((128, 256), alive).astype(jnp.bfloat16))
            target = jnp.concatenate(target, axis=0)
            for q in range(4):
                left = jnp.concatenate(
                    [rbuf[q * 8 : q * 8 + 8, i * 4 + k].reshape(256, 128) for k in range(4)], axis=1
                )
                mix[...] = jnp.dot(left, target, preferred_element_type=jnp.float32)
                for a in range(32):
                    row = psf[m, pl.ds(i * 128 + q * 32 + a, 1), :]
                    acc = acc + mix[a * 8 : a * 8 + 8, :] * row
            return acc

        return lax.fori_loop(0, 4, source, total)

    total = jnp.zeros((8, 256), jnp.float32)
    for m in range(3):
        for kind in ("L4", "S2"):
            if f"{kind}{m}" not in waited:
                take(f"{kind}{m}")
        for kind in ("W2", "W4", "WS"):
            arrived(f"{kind}{m}")
        total = component(m, total)

    mine = total * -cond_ref[...]
    weighted = mine[0:1] * gw_ref[0]
    for t in range(1, 8):
        weighted = weighted + mine[t : t + 1] * gw_ref[t]
    part[0:8] = mine
    part[8:16] = jnp.broadcast_to(weighted, (8, 256))
    gath[e] = part[...]
    for n, device in enumerate(peers):
        go(f"G{n}", part, gath.at[e], device)
    for n, device in enumerate(cross):
        go(f"H{n}", part.at[pl.ds(8, 8)], rows.at[e], device)
    for n in range(3):
        arrived(f"G{n}")
    for n in range(4):
        arrived(f"H{n}")
    grad_ref[...] = (gath[0, 0:8] + gath[1, 0:8]) + (gath[2, 0:8] + gath[3, 0:8])
    here = (gath[0, 8:9] + gath[1, 8:9]) + (gath[2, 8:9] + gath[3, 8:9])
    there = (rows[0, 0:1] + rows[1, 0:1]) + (rows[2, 0:1] + rows[3, 0:1])
    upd_ref[...] = here + there
    for copy in flying:
        copy.wait_send()


def per_device(panels, conductivity, residuals, gate_weight, pattern, live_count):
    vmem = pl.BlockSpec(memory_space=pltpu.VMEM)
    smem = pl.BlockSpec(memory_space=pltpu.SMEM)
    copies = 96
    grad, update = pl.pallas_call(
        kernel,
        out_shape=(
            jax.ShapeDtypeStruct((8, 256), jnp.float32),
            jax.ShapeDtypeStruct((1, 256), jnp.float32),
        ),
        in_specs=[pl.BlockSpec(memory_space=pl.ANY), vmem, vmem, smem, smem, smem],
        out_specs=(vmem, vmem),
        scratch_shapes=[
            pltpu.VMEM((32, 16, 32, 128), jnp.bfloat16),
            pltpu.VMEM((16, 128, 256), jnp.bfloat16),
            pltpu.VMEM((16, 128, 256), jnp.bfloat16),
            pltpu.VMEM((16, 128, 256), jnp.bfloat16),
            pltpu.VMEM((3, 3, 2, 128, 256), jnp.bfloat16),
            pltpu.VMEM((3, 512, 256), jnp.float32),
            pltpu.VMEM((256, 256), jnp.float32),
            pltpu.VMEM((16, 256), jnp.float32),
            pltpu.VMEM((4, 16, 256), jnp.float32),
            pltpu.VMEM((4, 8, 256), jnp.float32),
            pltpu.SemaphoreType.DMA((copies,)),
            pltpu.SemaphoreType.DMA((copies,)),
            pltpu.SemaphoreType.DMA((3,)),
        ],
        compiler_params=pltpu.CompilerParams(
            collective_id=0, has_side_effects=True, vmem_limit_bytes=40 << 20
        ),
        name="adjoint",
    )(
        panels.reshape(3, 4, 128, 256),
        residuals.reshape(512, 128),
        conductivity.reshape(1, 256),
        gate_weight,
        pattern,
        live_count,
    )
    return grad, update.reshape(256)


def solution(mesh):
    return jax.shard_map(
        per_device,
        mesh=mesh,
        in_specs=(
            P(None, "elec", "cell"),
            P("cell"),
            P("gate", "elec", None, "cell", None),
            P("gate"),
            P("elec", None),
            P("elec"),
        ),
        out_specs=(P("gate", "cell"), P("cell")),
        check_vma=False,
    )
```

```python
import jax
import jax.numpy as jnp
from jax import lax
from jax.experimental import pallas as pl
from jax.experimental.pallas import tpu as pltpu
from jax.sharding import PartitionSpec as P

MESH = pl.DeviceIdType.MESH
NX, NY, NZ = 4, 4, 8

NAMES = ["V0"]
for s in "UV":
    for way in "+-":
        NAMES += [s + "A" + way, s + "A2" + way]
        for gone in (0, 1, -1, 2):
            NAMES += [s + "B" + way + str(gone), s + "B2" + way + str(gone)]
for m in "012":
    for way in "ab":
        NAMES += [kind + m + way for kind in ("L1", "L2", "L3", "L4", "S1", "S2", "W2", "W4", "WS")]

PLAN = (
    0, 1, 11, 3, 13, 41, 50, 59, 68, 200, 77, 86, 100, 21, 31, 23, 33, 45, 54, 141, 150, 101, 111,
    103, 113, 5, 15, 2, 12, 42, 51, 159, 168, 60, 69, 177, 186, 7, 17, 78, 87, 121, 25, 35, 131,
    123, 133, 145, 154, 63, 72, 102, 112, 142, 47, 151, 27, 37, 56, 22, 32, 43, 52, 105, 115, 147,
    160, 65, 169, 74, 156, 9, 19, 61, 70, 165, 178, 83, 187, 24, 34, 92, 174, 125, 135, 46, 55, 107,
    117, 183, 163, 172, 26, 36, 192, 4, 14, 81, 79, 122, 132, 143, 152, 29, 39, 6, 16, 127, 137, 44,
    53, 161, 170, 8, 18, 124, 134, 90, 88, 109, 119, 146, 49, 155, 58, 28, 38, 10, 20, 126, 136, 62,
    64, 104, 114, 149, 179, 181, 158, 71, 73, 106, 116, 144, 48, 153, 57, 129, 30, 139, 40, 80, 82,
    108, 118, 148, 188, 190, 157, 128, 138, 89, 91, 110, 120, 162, 66, 164, 67, 166, 171, 75, 173,
    76, 167, 130, 140, 300, 301, 175, 302, 180, 84, 182, 85, 176, 303, 304, 189, 93, 191, 94, 184,
    305, 185, 306, 193, 307, 194, 308, 309, 310, 311,
)


def kernel(
    p_hbm, r_hbm, cond_ref, gw_ref, pat_ref, live_ref,
    grad_ref, upd_ref,
    rbuf, pall0, pall1, pall2, via, psf, res, mix, part, gath, rows, send, recv, local,
):
    pall = (pall0, pall1, pall2)
    cell = lax.axis_index("cell")
    e = lax.axis_index("elec")
    g = lax.axis_index("gate")
    y, x, zl = cell // (NX * 2), (cell // 2) % NX, cell % 2
    z = e * 2 + zl

    def cell_at(dx, dy, zlow):
        return (((y + dy + NY) % NY) * NX + (x + dx + NX) % NX) * 2 + zlow

    def xy(dx, dy):
        return {"cell": cell_at(dx, dy, zl), "elec": e, "gate": g}

    def at_z(dz, core=None):
        zz = (z + dz + 2 * NZ) % NZ
        return {"cell": cell_at(0, 0, zz % 2), "elec": zz // 2, "gate": g if core is None else core}

    z_mate = at_z(1 - 2 * zl)
    core_mate = {"cell": cell, "elec": e, "gate": 1 - g}
    peers = [at_z(d) for d in (2, 4, 6)]
    cross = [at_z(d, 1 - g) for d in (0, 2, 4, 6)]

    barrier = pltpu.get_barrier_semaphore()
    greet = [xy(1, 0), xy(-1, 0), xy(0, 1), xy(0, -1), at_z(1), at_z(-1)] + peers + cross
    for device in greet:
        pl.semaphore_signal(barrier, inc=1, device_id=device, device_id_type=MESH)

    fetch = pltpu.make_async_copy(r_hbm, res, local.at[3])
    fetch.start()
    own = [
        pltpu.make_async_copy(p_hbm.at[m], pall[m].at[pl.ds(e * 4, 4)], local.at[m])
        for m in range(3)
    ]
    for copy in own:
        copy.start()

    out_row = lax.broadcasted_iota(jnp.int32, (512, 512), 0)
    in_row = lax.broadcasted_iota(jnp.int32, (512, 512), 1)
    shuffle = jnp.where((out_row % 8) * 64 + out_row // 8 == in_row, 1.0, 0.0).astype(jnp.bfloat16)
    fetch.wait()
    turned = jnp.dot(shuffle, res[...], preferred_element_type=jnp.float32)
    rbuf[cell] = turned.astype(jnp.bfloat16).reshape(16, 32, 128)
    for copy in own:
        copy.wait()

    pl.semaphore_wait(barrier, len(greet))

    ids = {}
    copies = {}

    def go(name, src, dst, device):
        n = ids.setdefault(name, len(ids))
        copy = pltpu.make_async_remote_copy(
            src_ref=src, dst_ref=dst, send_sem=send.at[n], recv_sem=recv.at[n],
            device_id=device, device_id_type=MESH,
        )
        copy.start()
        copies[name] = copy

    def residual(name):
        if name == "V0":
            return go(name, rbuf.at[cell], rbuf.at[cell], z_mate)
        s, leg = name[0], name[1]
        second = name[2] == "2" and (leg == "A" or name[3] in "+-")
        sign = 1 if "+" == name[3 if second else 2] else -1
        gone = name[4 if second else 3 :]
        d1 = int(gone) if leg == "B" else 0
        d2 = 0
        if second and leg == "A":
            d1 = sign
        elif second:
            d2 = sign
        along_x = (leg == "A") == (s == "U")
        device = xy(sign, 0) if along_x else xy(0, sign)
        slot = cell_at(-d1, -d2, zl) if s == "U" else cell_at(-d2, -d1, 1 - zl)
        ref = rbuf.at[slot]
        if second:
            ref = rbuf.at[slot, pl.ds(0 if sign == 1 else 8, 8)]
        go(name, ref, ref, device)

    def panel(name):
        kind, m, up = name[:2], int(name[2]), name[3] == "a"
        sign = 1 if up else -1
        first = g * 2 + (0 if up else 1)

        def home(dz):
            return pall[m].at[pl.ds(((z + dz + 2 * NZ) % NZ) // 2 * 4 + first, 1)]

        def stop(n):
            return via.at[n, m, pl.ds(0 if up else 1, 1)]

        mine = home(0)
        if kind == "L1":
            go(name, mine, stop(0), at_z(sign))
        elif kind == "L2":
            go(name, stop(0), home(-sign), at_z(sign))
        elif kind == "L3":
            go(name, home(-2 * sign), stop(1), at_z(sign))
        elif kind == "L4":
            go(name, stop(1), home(-3 * sign), at_z(sign))
        elif kind == "S1":
            go(name, mine, stop(2), at_z(-sign))
        elif kind == "S2":
            go(name, stop(2), home(sign), at_z(-sign))
        else:
            ref = home({"W2": -2, "W4": 4, "WS": 2}[kind] * sign)
            go(name, ref, ref, core_mate)

    def component(m, i, total):
        target = []
        for k in range(4):
            there = pall[m][pat_ref[i, k]]
            alive = jnp.minimum(jnp.maximum(live_ref[i] - k, 0), 1).astype(jnp.float32)
            target.append(there * jnp.full((128, 256), alive).astype(jnp.bfloat16))
        target = jnp.concatenate(target, axis=0)
        for q in range(4):
            left = jnp.concatenate(
                [rbuf[q * 8 : q * 8 + 8, i * 4 + k].reshape(256, 128) for k in range(4)], axis=1
            )
            mix[...] = jnp.dot(left, target, preferred_element_type=jnp.float32)
            for a in range(32):
                row = psf[m, pl.ds(i * 128 + q * 32 + a, 1), :]
                total = total + mix[a * 8 : a * 8 + 8, :] * row
        return total

    total = jnp.zeros((8, 256), jnp.float32)
    for what in PLAN:
        kind, n = what // 100, what % 100
        if kind == 2:
            for m in range(3):
                psf[m] = pall[m][pl.ds(e * 4, 4)].reshape(512, 256).astype(jnp.float32)
        elif kind == 3:
            total = component(n // 4, n % 4, total)
        elif kind == 1:
            copies[NAMES[n]].wait_recv()
        elif NAMES[n][0] in "UV":
            residual(NAMES[n])
        else:
            panel(NAMES[n])

    mine = total * -cond_ref[...]
    weighted = mine[0:1] * gw_ref[0]
    for t in range(1, 8):
        weighted = weighted + mine[t : t + 1] * gw_ref[t]
    part[0:8] = mine
    part[8:16] = jnp.broadcast_to(weighted, (8, 256))
    for n, device in enumerate(peers):
        go(f"G{n}", part, gath.at[e], device)
    for n, device in enumerate(cross):
        go(f"H{n}", part.at[pl.ds(8, 8)], rows.at[e], device)
    gath[e] = part[...]
    for name in copies:
        if name[0] not in "GH":
            copies[name].wait_send()
    for name in copies:
        if name[0] in "GH":
            copies[name].wait_recv()
    grad_ref[...] = (gath[0, 0:8] + gath[1, 0:8]) + (gath[2, 0:8] + gath[3, 0:8])
    here = (gath[0, 8:9] + gath[1, 8:9]) + (gath[2, 8:9] + gath[3, 8:9])
    there = (rows[0, 0:1] + rows[1, 0:1]) + (rows[2, 0:1] + rows[3, 0:1])
    upd_ref[...] = here + there
    for name in copies:
        if name[0] in "GH":
            copies[name].wait_send()


def per_device(panels, conductivity, residuals, gate_weight, pattern, live_count):
    vmem = pl.BlockSpec(memory_space=pltpu.VMEM)
    smem = pl.BlockSpec(memory_space=pltpu.SMEM)
    hbm = pl.BlockSpec(memory_space=pl.ANY)
    copies = 112
    grad, update = pl.pallas_call(
        kernel,
        out_shape=(
            jax.ShapeDtypeStruct((8, 256), jnp.float32),
            jax.ShapeDtypeStruct((1, 256), jnp.float32),
        ),
        in_specs=[hbm, hbm, vmem, smem, smem, smem],
        out_specs=(vmem, vmem),
        scratch_shapes=[
            pltpu.VMEM((32, 16, 32, 128), jnp.bfloat16),
            pltpu.VMEM((16, 128, 256), jnp.bfloat16),
            pltpu.VMEM((16, 128, 256), jnp.bfloat16),
            pltpu.VMEM((16, 128, 256), jnp.bfloat16),
            pltpu.VMEM((3, 3, 2, 128, 256), jnp.bfloat16),
            pltpu.VMEM((3, 512, 256), jnp.float32),
            pltpu.VMEM((512, 128), jnp.bfloat16),
            pltpu.VMEM((256, 256), jnp.float32),
            pltpu.VMEM((16, 256), jnp.float32),
            pltpu.VMEM((4, 16, 256), jnp.float32),
            pltpu.VMEM((4, 8, 256), jnp.float32),
            pltpu.SemaphoreType.DMA((copies,)),
            pltpu.SemaphoreType.DMA((copies,)),
            pltpu.SemaphoreType.DMA((4,)),
        ],
        compiler_params=pltpu.CompilerParams(
            collective_id=0, has_side_effects=True, vmem_limit_bytes=63 << 20
        ),
        name="adjoint",
    )(
        panels.reshape(3, 4, 128, 256),
        residuals.reshape(512, 128),
        conductivity.reshape(1, 256),
        gate_weight,
        pattern,
        live_count,
    )
    return grad, update.reshape(256)


def solution(mesh):
    return jax.shard_map(
        per_device,
        mesh=mesh,
        in_specs=(
            P(None, "elec", "cell"),
            P("cell"),
            P("gate", "elec", None, "cell", None),
            P("gate"),
            P("elec", None),
            P("elec"),
        ),
        out_specs=(P("gate", "cell"), P("cell")),
        check_vma=False,
    )
```

```python
import jax
import jax.numpy as jnp
from jax import lax
from jax.experimental import pallas as pl
from jax.experimental.pallas import tpu as pltpu
from jax.sharding import PartitionSpec as P

MESH = pl.DeviceIdType.MESH
NX, NY, NZ = 4, 4, 8

NAMES = ["V0"]
for s in "UV":
    for way in "+-":
        NAMES += [s + "A" + way, s + "A2" + way]
        for gone in (0, 1, -1, 2):
            NAMES += [s + "B" + way + str(gone), s + "B2" + way + str(gone)]
for m in "012":
    for way in "ab":
        NAMES += [kind + m + way for kind in ("L1", "L2", "L3", "L4", "S1", "S2", "W2", "W4", "WS")]

PLAN = (
    0, 1, 11, 3, 13, 41, 50, 59, 68, 200, 77, 86, 100, 21, 31, 23, 33, 45, 54, 141, 150, 101, 111,
    103, 113, 5, 15, 2, 12, 42, 51, 159, 168, 60, 69, 177, 186, 7, 17, 78, 87, 121, 25, 35, 131,
    123, 133, 145, 154, 63, 72, 102, 112, 142, 47, 151, 27, 37, 56, 22, 32, 43, 52, 105, 115, 147,
    160, 65, 169, 74, 156, 9, 19, 61, 70, 165, 178, 83, 187, 24, 34, 92, 174, 125, 135, 46, 55, 107,
    117, 183, 163, 172, 26, 36, 192, 4, 14, 81, 79, 122, 132, 143, 152, 29, 39, 6, 16, 127, 137, 44,
    53, 161, 170, 8, 18, 124, 134, 90, 88, 109, 119, 146, 49, 155, 58, 28, 38, 10, 20, 126, 136, 62,
    64, 104, 114, 149, 179, 181, 158, 71, 73, 106, 116, 144, 48, 153, 57, 129, 30, 139, 40, 80, 82,
    108, 118, 148, 188, 190, 157, 128, 138, 89, 91, 110, 120, 162, 66, 164, 67, 166, 171, 75, 173,
    76, 167, 130, 140, 300, 301, 302, 175, 303, 180, 84, 182, 85, 176, 304, 305, 306, 307, 184, 189,
    93, 191, 94, 185, 193, 194, 308, 309, 310, 311,
)


def kernel(
    p_hbm, r_hbm, cond_hbm, gw_hbm, pat_hbm, live_hbm,
    grad_ref, upd_ref,
    cond_ref, gw_ref, pat_ref, live_ref, rbuf, pall0, pall1, pall2, via, psf, res, mix, part, row, gath, rows, send, recv, local,
):
    pall = (pall0, pall1, pall2)
    cell = lax.axis_index("cell")
    e = lax.axis_index("elec")
    g = lax.axis_index("gate")
    y, x, zl = cell // (NX * 2), (cell // 2) % NX, cell % 2
    z = e * 2 + zl

    def cell_at(dx, dy, zlow):
        return (((y + dy + NY) % NY) * NX + (x + dx + NX) % NX) * 2 + zlow

    def xy(dx, dy):
        return {"cell": cell_at(dx, dy, zl), "elec": e, "gate": g}

    def at_z(dz, core=None):
        zz = (z + dz + 2 * NZ) % NZ
        return {"cell": cell_at(0, 0, zz % 2), "elec": zz // 2, "gate": g if core is None else core}

    z_mate = at_z(1 - 2 * zl)
    core_mate = {"cell": cell, "elec": e, "gate": 1 - g}
    peers = [at_z(d) for d in (2, 4, 6)]
    cross = [at_z(d, 1 - g) for d in (0, 2, 4, 6)]

    barrier = pltpu.get_barrier_semaphore()
    greet = [xy(1, 0), xy(-1, 0), xy(0, 1), xy(0, -1), at_z(1), at_z(-1)] + peers + cross
    for device in greet:
        pl.semaphore_signal(barrier, inc=1, device_id=device, device_id_type=MESH)

    fetch = pltpu.make_async_copy(r_hbm, res, local.at[3])
    fetch.start()
    own = [
        pltpu.make_async_copy(p_hbm.at[m], pall[m].at[pl.ds(e * 4, 4)], local.at[m])
        for m in range(3)
    ]
    own += [
        pltpu.make_async_copy(src, dst, local.at[4 + n])
        for n, (src, dst) in enumerate(
            ((cond_hbm, cond_ref), (gw_hbm, gw_ref), (pat_hbm, pat_ref), (live_hbm, live_ref))
        )
    ]
    for copy in own:
        copy.start()

    out_row = lax.broadcasted_iota(jnp.int32, (512, 512), 0)
    in_row = lax.broadcasted_iota(jnp.int32, (512, 512), 1)
    shuffle = jnp.where((out_row % 8) * 64 + out_row // 8 == in_row, 1.0, 0.0).astype(jnp.bfloat16)
    fetch.wait()
    turned = jnp.dot(shuffle, res[...], preferred_element_type=jnp.float32)
    rbuf[cell] = turned.astype(jnp.bfloat16).reshape(16, 32, 128)
    for copy in own:
        copy.wait()

    pl.semaphore_wait(barrier, len(greet))

    ids = {}
    copies = {}

    def go(name, src, dst, device):
        n = ids.setdefault(name, len(ids))
        copy = pltpu.make_async_remote_copy(
            src_ref=src, dst_ref=dst, send_sem=send.at[n], recv_sem=recv.at[n],
            device_id=device, device_id_type=MESH,
        )
        copy.start()
        copies[name] = copy

    def residual(name):
        if name == "V0":
            return go(name, rbuf.at[cell], rbuf.at[cell], z_mate)
        s, leg = name[0], name[1]
        second = name[2] == "2" and (leg == "A" or name[3] in "+-")
        sign = 1 if "+" == name[3 if second else 2] else -1
        gone = name[4 if second else 3 :]
        d1 = int(gone) if leg == "B" else 0
        d2 = 0
        if second and leg == "A":
            d1 = sign
        elif second:
            d2 = sign
        along_x = (leg == "A") == (s == "U")
        device = xy(sign, 0) if along_x else xy(0, sign)
        slot = cell_at(-d1, -d2, zl) if s == "U" else cell_at(-d2, -d1, 1 - zl)
        ref = rbuf.at[slot]
        if second:
            ref = rbuf.at[slot, pl.ds(0 if sign == 1 else 8, 8)]
        go(name, ref, ref, device)

    def panel(name):
        kind, m, up = name[:2], int(name[2]), name[3] == "a"
        sign = 1 if up else -1
        first = g * 2 + (0 if up else 1)

        def home(dz):
            return pall[m].at[pl.ds(((z + dz + 2 * NZ) % NZ) // 2 * 4 + first, 1)]

        def stop(n):
            return via.at[n, m, pl.ds(0 if up else 1, 1)]

        mine = home(0)
        if kind == "L1":
            go(name, mine, stop(0), at_z(sign))
        elif kind == "L2":
            go(name, stop(0), home(-sign), at_z(sign))
        elif kind == "L3":
            go(name, home(-2 * sign), stop(1), at_z(sign))
        elif kind == "L4":
            go(name, stop(1), home(-3 * sign), at_z(sign))
        elif kind == "S1":
            go(name, mine, stop(2), at_z(-sign))
        elif kind == "S2":
            go(name, stop(2), home(sign), at_z(-sign))
        else:
            ref = home({"W2": -2, "W4": 4, "WS": 2}[kind] * sign)
            go(name, ref, ref, core_mate)

    def component(m, i, total):
        target = []
        for k in range(4):
            there = pall[m][pat_ref[i, k]]
            alive = jnp.minimum(jnp.maximum(live_ref[i] - k, 0), 1).astype(jnp.float32)
            target.append(there * jnp.full((128, 256), alive).astype(jnp.bfloat16))
        target = jnp.concatenate(target, axis=0)
        for q in range(4):
            left = jnp.concatenate(
                [rbuf[q * 8 : q * 8 + 8, i * 4 + k].reshape(256, 128) for k in range(4)], axis=1
            )
            mix[...] = jnp.dot(left, target, preferred_element_type=jnp.float32)
            for a in range(32):
                source = psf[m, pl.ds(i * 128 + q * 32 + a, 1), :]
                total = total + mix[a * 8 : a * 8 + 8, :] * source
        return total

    total = jnp.zeros((8, 256), jnp.float32)
    for what in PLAN:
        kind, n = what // 100, what % 100
        if kind == 2:
            for m in range(3):
                psf[m] = pall[m][pl.ds(e * 4, 4)].reshape(512, 256).astype(jnp.float32)
        elif kind == 3:
            total = component(n // 4, n % 4, total)
        elif kind == 1:
            copies[NAMES[n]].wait_recv()
        elif NAMES[n][0] in "UV":
            residual(NAMES[n])
        else:
            panel(NAMES[n])

    mine = total * -cond_ref[...]
    weighted = mine[0:1] * gw_ref[0]
    for t in range(1, 8):
        weighted = weighted + mine[t : t + 1] * gw_ref[t]
    part[...] = mine
    row[...] = weighted
    for n, device in enumerate(peers):
        go(f"G{n}", part, gath.at[e], device)
    for n, device in enumerate(peers):
        go(f"H{n}", row, rows.at[g, e], device)
    for n, device in enumerate(cross):
        go(f"I{n}", row, rows.at[g, e], device)
    gath[e] = mine
    rows[g, e] = weighted
    for name in copies:
        if name[0] not in "GHI":
            copies[name].wait_send()
    for name in copies:
        if name[0] in "GHI":
            copies[name].wait_recv()
    grad_ref[...] = (gath[0] + gath[1]) + (gath[2] + gath[3])
    each = [(rows[n, 0] + rows[n, 1]) + (rows[n, 2] + rows[n, 3]) for n in range(2)]
    upd_ref[...] = each[0] + each[1]
    for name in copies:
        if name[0] in "GHI":
            copies[name].wait_send()


def per_device(panels, conductivity, residuals, gate_weight, pattern, live_count):
    vmem = pl.BlockSpec(memory_space=pltpu.VMEM)
    hbm = pl.BlockSpec(memory_space=pl.ANY)
    copies = 112
    grad, update = pl.pallas_call(
        kernel,
        out_shape=(
            pltpu.VMEM((8, 256), jnp.float32),
            pltpu.VMEM((1, 256), jnp.float32),
        ),
        in_specs=[hbm] * 6,
        out_specs=(vmem, vmem),
        scratch_shapes=[
            pltpu.VMEM((1, 256), jnp.float32),
            pltpu.SMEM((8,), jnp.float32),
            pltpu.SMEM((4, 4), jnp.int32),
            pltpu.SMEM((4,), jnp.int32),
            pltpu.VMEM((32, 16, 32, 128), jnp.bfloat16),
            pltpu.VMEM((16, 128, 256), jnp.bfloat16),
            pltpu.VMEM((16, 128, 256), jnp.bfloat16),
            pltpu.VMEM((16, 128, 256), jnp.bfloat16),
            pltpu.VMEM((3, 3, 2, 128, 256), jnp.bfloat16),
            pltpu.VMEM((3, 512, 256), jnp.float32),
            pltpu.VMEM((512, 128), jnp.bfloat16),
            pltpu.VMEM((256, 256), jnp.float32),
            pltpu.VMEM((8, 256), jnp.float32),
            pltpu.VMEM((1, 256), jnp.float32),
            pltpu.VMEM((4, 8, 256), jnp.float32),
            pltpu.VMEM((2, 4, 1, 256), jnp.float32),
            pltpu.SemaphoreType.DMA((copies,)),
            pltpu.SemaphoreType.DMA((copies,)),
            pltpu.SemaphoreType.DMA((8,)),
        ],
        compiler_params=pltpu.CompilerParams(
            collective_id=0, has_side_effects=True, vmem_limit_bytes=60 << 20
        ),
        name="adjoint",
    )(
        panels.reshape(3, 4, 128, 256),
        residuals.reshape(512, 128),
        conductivity.reshape(1, 256),
        gate_weight,
        pattern,
        live_count,
    )
    return grad, update.reshape(256)


def solution(mesh):
    return jax.shard_map(
        per_device,
        mesh=mesh,
        in_specs=(
            P(None, "elec", "cell"),
            P("cell"),
            P("gate", "elec", None, "cell", None),
            P("gate"),
            P("elec", None),
            P("elec"),
        ),
        out_specs=(P("gate", "cell"), P("cell")),
        check_vma=False,
    )
```

```python
import jax
import jax.numpy as jnp
from jax import lax
from jax.experimental import pallas as pl
from jax.experimental.pallas import tpu as pltpu
from jax.sharding import PartitionSpec as P

MESH = pl.DeviceIdType.MESH
NX, NY, NZ = 4, 4, 8

NAMES = ["V0"]
for s in "UV":
    for way in "+-":
        NAMES += [s + "A" + way, s + "C" + way, s + "A2" + way]
        for gone in (0, 1, -1, 2):
            NAMES += [s + kind + way + str(gone) for kind in ("B", "D", "B2")]
for m in "012":
    for way in "ab":
        NAMES += [kind + m + way for kind in ("L1", "L2", "L3", "L4", "S1", "S2", "W2", "W4", "WS")]

PLAN = (
    0, 1, 17, 4, 20, 61, 70, 2, 16, 5, 19, 400, 79, 88, 97, 106, 200, 31, 47, 34, 50, 201, 217, 204,
    220, 32, 46, 3, 18, 65, 74, 261, 270, 202, 216, 205, 219, 7, 23, 35, 49, 62, 71, 279, 288, 10,
    26, 80, 89, 231, 37, 52, 247, 234, 250, 297, 306, 33, 48, 41, 56, 98, 107, 232, 246, 203, 218,
    265, 274, 13, 29, 40, 53, 83, 92, 207, 223, 235, 249, 262, 67, 271, 76, 8, 22, 38, 55, 63, 72,
    210, 226, 237, 252, 267, 280, 85, 289, 94, 276, 11, 25, 36, 51, 81, 90, 233, 248, 241, 256, 285,
    298, 103, 307, 112, 294, 14, 28, 43, 59, 66, 75, 213, 229, 240, 253, 303, 283, 292, 312, 6, 21,
    44, 58, 101, 99, 208, 222, 238, 255, 263, 272, 9, 24, 39, 54, 64, 73, 211, 225, 236, 251, 281,
    290, 12, 27, 42, 57, 110, 108, 214, 228, 243, 259, 266, 69, 275, 78, 15, 30, 45, 60, 82, 84,
    206, 221, 244, 258, 269, 299, 301, 278, 91, 93, 209, 224, 239, 254, 264, 68, 273, 77, 100, 102,
    212, 227, 242, 257, 268, 308, 310, 277, 109, 111, 215, 230, 245, 260, 600, 282, 86, 284, 87,
    601, 602, 603, 286, 291, 95, 293, 96, 287, 295, 300, 104, 302, 105, 296, 604, 605, 606, 607,
    304, 309, 113, 311, 114, 305, 313, 314, 608, 609, 610, 611,
)


def kernel(
    p_hbm, r_hbm, cond_hbm, gw_hbm, pat_hbm, live_hbm,
    grad_ref, upd_ref,
    cond_ref, gw_ref, pat_ref, live_ref, rbuf, pall0, pall1, pall2, via, psf, res, mix, part, row, gath, rows, send, recv, local,
):
    pall = (pall0, pall1, pall2)
    cell = lax.axis_index("cell")
    e = lax.axis_index("elec")
    g = lax.axis_index("gate")
    y, x, zl = cell // (NX * 2), (cell // 2) % NX, cell % 2
    z = e * 2 + zl

    def cell_at(dx, dy, zlow):
        return (((y + dy + NY) % NY) * NX + (x + dx + NX) % NX) * 2 + zlow

    def xy(dx, dy):
        return {"cell": cell_at(dx, dy, zl), "elec": e, "gate": g}

    def at_z(dz, core=None):
        zz = (z + dz + 2 * NZ) % NZ
        return {"cell": cell_at(0, 0, zz % 2), "elec": zz // 2, "gate": g if core is None else core}

    z_mate = at_z(1 - 2 * zl)
    core_mate = {"cell": cell, "elec": e, "gate": 1 - g}
    peers = [at_z(d) for d in (4, 2, 6)]
    cross = [at_z(d, 1 - g) for d in (4, 2, 6, 0)]

    barrier = pltpu.get_barrier_semaphore()
    greet = [xy(1, 0), xy(-1, 0), xy(0, 1), xy(0, -1), at_z(1), at_z(-1), core_mate]
    for device in greet:
        pl.semaphore_signal(barrier, inc=1, device_id=device, device_id_type=MESH)

    fetch = pltpu.make_async_copy(r_hbm, res, local.at[3])
    fetch.start()
    own = [
        pltpu.make_async_copy(p_hbm.at[m], pall[m].at[pl.ds(e * 4, 4)], local.at[m])
        for m in range(3)
    ]
    own += [
        pltpu.make_async_copy(src, dst, local.at[4 + n])
        for n, (src, dst) in enumerate(
            ((cond_hbm, cond_ref), (gw_hbm, gw_ref), (pat_hbm, pat_ref), (live_hbm, live_ref))
        )
    ]
    for copy in own:
        copy.start()

    out_row = lax.broadcasted_iota(jnp.int32, (512, 512), 0)
    in_row = lax.broadcasted_iota(jnp.int32, (512, 512), 1)
    shuffle = jnp.where((out_row % 8) * 64 + out_row // 8 == in_row, 1.0, 0.0).astype(jnp.bfloat16)
    fetch.wait()
    turned = jnp.dot(shuffle, res[...], preferred_element_type=jnp.float32)
    rbuf[cell] = turned.astype(jnp.bfloat16).reshape(16, 32, 128)
    for copy in own:
        copy.wait()

    pl.semaphore_wait(barrier, len(greet))

    ids = {}
    copies = {}

    def go(name, src, dst, device):
        n = ids.setdefault(name, len(ids))
        copy = pltpu.make_async_remote_copy(
            src_ref=src, dst_ref=dst, send_sem=send.at[n], recv_sem=recv.at[n],
            device_id=device, device_id_type=MESH,
        )
        copy.start()
        copies[name] = copy

    def residual(name):
        if name == "V0":
            return go(name, rbuf.at[cell], rbuf.at[cell], z_mate)
        s, leg = name[0], name[1]
        second = name[2] == "2"
        sign = 1 if name[3 if second else 2] == "+" else -1
        gone = name[4 if second else 3 :]
        first_axis = leg in "AC"
        half = (0 if sign == 1 else 1) if second else (0 if leg in "AB" else 1)
        d1 = (sign if second else 0) if first_axis else int(gone)
        d2 = sign if second and not first_axis else 0
        device = xy(sign, 0) if first_axis == (s == "U") else xy(0, sign)
        slot = cell_at(-d1, -d2, zl) if s == "U" else cell_at(-d2, -d1, 1 - zl)
        ref = rbuf.at[slot, pl.ds(half * 8, 8)]
        go(name, ref, ref, device)

    def panel(name):
        kind, m, up = name[:2], int(name[2]), name[3] == "a"
        sign = 1 if up else -1
        first = g * 2 + (0 if up else 1)

        def home(dz):
            return pall[m].at[pl.ds(((z + dz + 2 * NZ) % NZ) // 2 * 4 + first, 1)]

        def stop(n):
            return via.at[n, m, pl.ds(0 if up else 1, 1)]

        mine = home(0)
        if kind == "L1":
            go(name, mine, stop(0), at_z(sign))
        elif kind == "L2":
            go(name, stop(0), home(-sign), at_z(sign))
        elif kind == "L3":
            go(name, home(-2 * sign), stop(1), at_z(sign))
        elif kind == "L4":
            go(name, stop(1), home(-3 * sign), at_z(sign))
        elif kind == "S1":
            go(name, mine, stop(2), at_z(-sign))
        elif kind == "S2":
            go(name, stop(2), home(sign), at_z(-sign))
        else:
            ref = home({"W2": -2, "W4": 4, "WS": 2}[kind] * sign)
            go(name, ref, ref, core_mate)

    def component(m, i, total):
        target = []
        for k in range(4):
            there = pall[m][pat_ref[i, k]]
            alive = jnp.minimum(jnp.maximum(live_ref[i] - k, 0), 1).astype(jnp.float32)
            target.append(there * jnp.full((128, 256), alive).astype(jnp.bfloat16))
        target = jnp.concatenate(target, axis=0)
        for q in range(4):
            left = jnp.concatenate(
                [rbuf[q * 8 : q * 8 + 8, i * 4 + k].reshape(256, 128) for k in range(4)], axis=1
            )
            mix[...] = jnp.dot(left, target, preferred_element_type=jnp.float32)
            for a in range(32):
                source = psf[m, pl.ds(i * 128 + q * 32 + a, 1), :]
                total = total + mix[a * 8 : a * 8 + 8, :] * source
        return total

    total = jnp.zeros((8, 256), jnp.float32)
    for what in PLAN:
        kind, n = what // 200, what % 200
        if kind == 2:
            for m in range(3):
                psf[m] = pall[m][pl.ds(e * 4, 4)].reshape(512, 256).astype(jnp.float32)
        elif kind == 3:
            total = component(n // 4, n % 4, total)
        elif kind == 1:
            copies[NAMES[n]].wait_recv()
        elif NAMES[n][0] in "UV":
            residual(NAMES[n])
        else:
            panel(NAMES[n])

    mine = total * -cond_ref[...]
    weighted = mine[0:1] * gw_ref[0]
    for t in range(1, 8):
        weighted = weighted + mine[t : t + 1] * gw_ref[t]
    part[...] = mine
    row[...] = weighted
    for n, device in enumerate(peers):
        go(f"G{n}", part, gath.at[e], device)
    for n, device in enumerate(peers):
        go(f"H{n}", row, rows.at[g, e], device)
    for n, device in enumerate(cross):
        go(f"I{n}", row, rows.at[g, e], device)
    gath[e] = mine
    rows[g, e] = weighted
    for name in copies:
        if name[0] not in "GHI":
            copies[name].wait_send()
    for name in copies:
        if name[0] in "GHI":
            copies[name].wait_recv()
    grad_ref[...] = (gath[0] + gath[1]) + (gath[2] + gath[3])
    each = [(rows[n, 0] + rows[n, 1]) + (rows[n, 2] + rows[n, 3]) for n in range(2)]
    upd_ref[...] = each[0] + each[1]
    for name in copies:
        if name[0] in "GHI":
            copies[name].wait_send()


def per_device(panels, conductivity, residuals, gate_weight, pattern, live_count):
    vmem = pl.BlockSpec(memory_space=pltpu.VMEM)
    hbm = pl.BlockSpec(memory_space=pl.ANY)
    copies = 128
    grad, update = pl.pallas_call(
        kernel,
        out_shape=(
            pltpu.VMEM((8, 256), jnp.float32),
            pltpu.VMEM((1, 256), jnp.float32),
        ),
        in_specs=[hbm] * 6,
        out_specs=(vmem, vmem),
        scratch_shapes=[
            pltpu.VMEM((1, 256), jnp.float32),
            pltpu.SMEM((8,), jnp.float32),
            pltpu.SMEM((4, 4), jnp.int32),
            pltpu.SMEM((4,), jnp.int32),
            pltpu.VMEM((32, 16, 32, 128), jnp.bfloat16),
            pltpu.VMEM((16, 128, 256), jnp.bfloat16),
            pltpu.VMEM((16, 128, 256), jnp.bfloat16),
            pltpu.VMEM((16, 128, 256), jnp.bfloat16),
            pltpu.VMEM((3, 3, 2, 128, 256), jnp.bfloat16),
            pltpu.VMEM((3, 512, 256), jnp.float32),
            pltpu.VMEM((512, 128), jnp.bfloat16),
            pltpu.VMEM((256, 256), jnp.float32),
            pltpu.VMEM((8, 256), jnp.float32),
            pltpu.VMEM((1, 256), jnp.float32),
            pltpu.VMEM((4, 8, 256), jnp.float32),
            pltpu.VMEM((2, 4, 1, 256), jnp.float32),
            pltpu.SemaphoreType.DMA((copies,)),
            pltpu.SemaphoreType.DMA((copies,)),
            pltpu.SemaphoreType.DMA((8,)),
        ],
        compiler_params=pltpu.CompilerParams(
            collective_id=0, has_side_effects=True, vmem_limit_bytes=60 << 20
        ),
        name="adjoint",
    )(
        panels.reshape(3, 4, 128, 256),
        residuals.reshape(512, 128),
        conductivity.reshape(1, 256),
        gate_weight,
        pattern,
        live_count,
    )
    return grad, update.reshape(256)


def solution(mesh):
    return jax.shard_map(
        per_device,
        mesh=mesh,
        in_specs=(
            P(None, "elec", "cell"),
            P("cell"),
            P("gate", "elec", None, "cell", None),
            P("gate"),
            P("elec", None),
            P("elec"),
        ),
        out_specs=(P("gate", "cell"), P("cell")),
        check_vma=False,
    )
```

```python
import jax
import jax.numpy as jnp
from jax import lax
from jax.experimental import pallas as pl
from jax.experimental.pallas import tpu as pltpu
from jax.sharding import PartitionSpec as P

MESH = pl.DeviceIdType.MESH
NX, NY, NZ = 4, 4, 8

NAMES = ["V0"]
for s in "UV":
    for way in "+-":
        NAMES += [s + "A" + way, s + "C" + way, s + "A2" + way]
        for gone in (0, 1, -1, 2):
            NAMES += [s + kind + way + str(gone) for kind in ("B", "D", "B2")]
for m in "012":
    for way in "ab":
        NAMES += [kind + m + way for kind in ("L1", "L2", "L3", "L4", "S1", "S2", "W2", "W4", "WS")]

PLAN = (
    0, 1, 17, 4, 20, 61, 70, 2, 16, 5, 19, 400, 79, 88, 97, 106, 200, 31, 47, 34, 50, 201, 217, 204,
    220, 32, 46, 3, 18, 65, 74, 261, 270, 202, 216, 205, 219, 7, 23, 35, 49, 62, 71, 279, 288, 10,
    26, 80, 89, 231, 37, 52, 247, 234, 250, 297, 306, 33, 48, 41, 56, 98, 107, 232, 246, 203, 218,
    265, 274, 13, 29, 40, 53, 83, 92, 207, 223, 235, 249, 262, 67, 271, 76, 8, 22, 38, 55, 63, 72,
    210, 226, 237, 252, 267, 280, 85, 289, 94, 276, 11, 25, 36, 51, 81, 90, 233, 248, 241, 256, 285,
    298, 103, 307, 112, 294, 14, 28, 43, 59, 66, 75, 213, 229, 240, 253, 303, 283, 292, 312, 6, 21,
    44, 58, 101, 99, 208, 222, 238, 255, 263, 272, 9, 24, 39, 54, 64, 73, 211, 225, 236, 251, 281,
    290, 12, 27, 42, 57, 110, 108, 214, 228, 243, 259, 266, 69, 275, 78, 15, 30, 45, 60, 82, 84,
    206, 221, 244, 258, 269, 299, 301, 278, 91, 93, 209, 224, 239, 254, 264, 68, 273, 77, 100, 102,
    212, 227, 242, 257, 268, 308, 310, 277, 109, 111, 215, 230, 245, 260, 282, 86, 284, 87, 600,
    601, 602, 603, 286, 291, 95, 293, 96, 287, 300, 104, 302, 105, 295, 296, 604, 605, 606, 607,
    304, 309, 113, 311, 114, 305, 313, 314, 608, 609, 610, 611,
)


def kernel(
    p_hbm, r_hbm, cond_hbm, gw_hbm, pat_hbm, live_hbm,
    grad_ref, upd_ref,
    cond_ref, gw_ref, pat_ref, live_ref, rbuf, pall0, pall1, pall2, via, psf, res, mix, part, row, gath, rows, send, recv, local,
):
    pall = (pall0, pall1, pall2)
    cell = lax.axis_index("cell")
    e = lax.axis_index("elec")
    g = lax.axis_index("gate")
    y, x, zl = cell // (NX * 2), (cell // 2) % NX, cell % 2
    z = e * 2 + zl

    def cell_at(dx, dy, zlow):
        return (((y + dy + NY) % NY) * NX + (x + dx + NX) % NX) * 2 + zlow

    def xy(dx, dy):
        return {"cell": cell_at(dx, dy, zl), "elec": e, "gate": g}

    def at_z(dz, core=None):
        zz = (z + dz + 2 * NZ) % NZ
        return {"cell": cell_at(0, 0, zz % 2), "elec": zz // 2, "gate": g if core is None else core}

    z_mate = at_z(1 - 2 * zl)
    core_mate = {"cell": cell, "elec": e, "gate": 1 - g}
    peers = [at_z(d) for d in (4, 2, 6)]
    cross = [at_z(d, 1 - g) for d in (4, 2, 6, 0)]

    barrier = pltpu.get_barrier_semaphore()
    greet = [xy(1, 0), xy(-1, 0), xy(0, 1), xy(0, -1), at_z(1), at_z(-1), core_mate]
    for device in greet:
        pl.semaphore_signal(barrier, inc=1, device_id=device, device_id_type=MESH)

    fetch = pltpu.make_async_copy(r_hbm, res, local.at[3])
    fetch.start()
    own = [
        pltpu.make_async_copy(p_hbm.at[m], pall[m].at[pl.ds(e * 4, 4)], local.at[m])
        for m in range(3)
    ]
    own += [
        pltpu.make_async_copy(src, dst, local.at[4 + n])
        for n, (src, dst) in enumerate(
            ((cond_hbm, cond_ref), (gw_hbm, gw_ref), (pat_hbm, pat_ref), (live_hbm, live_ref))
        )
    ]
    for copy in own:
        copy.start()

    out_row = lax.broadcasted_iota(jnp.int32, (512, 512), 0)
    in_row = lax.broadcasted_iota(jnp.int32, (512, 512), 1)
    shuffle = jnp.where((out_row % 8) * 64 + out_row // 8 == in_row, 1.0, 0.0).astype(jnp.bfloat16)
    fetch.wait()
    turned = jnp.dot(shuffle, res[...], preferred_element_type=jnp.float32)
    rbuf[cell] = turned.astype(jnp.bfloat16).reshape(16, 32, 128)
    pl.semaphore_wait(barrier, len(greet))

    ids = {}
    copies = {}

    def go(name, src, dst, device):
        n = ids.setdefault(name, len(ids))
        copy = pltpu.make_async_remote_copy(
            src_ref=src, dst_ref=dst, send_sem=send.at[n], recv_sem=recv.at[n],
            device_id=device, device_id_type=MESH,
        )
        copy.start()
        copies[name] = copy

    def residual(name):
        if name == "V0":
            return go(name, rbuf.at[cell], rbuf.at[cell], z_mate)
        s, leg = name[0], name[1]
        second = name[2] == "2"
        sign = 1 if name[3 if second else 2] == "+" else -1
        gone = name[4 if second else 3 :]
        first_axis = leg in "AC"
        half = (0 if sign == 1 else 1) if second else (0 if leg in "AB" else 1)
        d1 = (sign if second else 0) if first_axis else int(gone)
        d2 = sign if second and not first_axis else 0
        device = xy(sign, 0) if first_axis == (s == "U") else xy(0, sign)
        slot = cell_at(-d1, -d2, zl) if s == "U" else cell_at(-d2, -d1, 1 - zl)
        ref = rbuf.at[slot, pl.ds(half * 8, 8)]
        go(name, ref, ref, device)

    def panel(name):
        kind, m, up = name[:2], int(name[2]), name[3] == "a"
        sign = 1 if up else -1
        first = g * 2 + (0 if up else 1)

        def home(dz):
            return pall[m].at[pl.ds(((z + dz + 2 * NZ) % NZ) // 2 * 4 + first, 1)]

        def stop(n):
            return via.at[n, m, pl.ds(0 if up else 1, 1)]

        mine = p_hbm.at[m, pl.ds(first, 1)]
        if kind == "L1":
            go(name, mine, stop(0), at_z(sign))
        elif kind == "L2":
            go(name, stop(0), home(-sign), at_z(sign))
        elif kind == "L3":
            go(name, home(-2 * sign), stop(1), at_z(sign))
        elif kind == "L4":
            go(name, stop(1), home(-3 * sign), at_z(sign))
        elif kind == "S1":
            go(name, mine, stop(2), at_z(-sign))
        elif kind == "S2":
            go(name, stop(2), home(sign), at_z(-sign))
        else:
            ref = home({"W2": -2, "W4": 4, "WS": 2}[kind] * sign)
            go(name, ref, ref, core_mate)

    def component(m, i, total):
        target = []
        for k in range(4):
            there = pall[m][pat_ref[i, k]]
            alive = jnp.minimum(jnp.maximum(live_ref[i] - k, 0), 1).astype(jnp.float32)
            target.append(there * jnp.full((128, 256), alive).astype(jnp.bfloat16))
        target = jnp.concatenate(target, axis=0)
        for q in range(4):
            left = jnp.concatenate(
                [rbuf[q * 8 : q * 8 + 8, i * 4 + k].reshape(256, 128) for k in range(4)], axis=1
            )
            mix[...] = jnp.dot(left, target, preferred_element_type=jnp.float32)
            for a in range(32):
                source = psf[m, pl.ds(i * 128 + q * 32 + a, 1), :]
                total = total + mix[a * 8 : a * 8 + 8, :] * source
        return total

    total = jnp.zeros((8, 256), jnp.float32)
    for what in PLAN:
        kind, n = what // 200, what % 200
        if kind == 2:
            for copy in own:
                copy.wait()
            for m in range(3):
                psf[m] = pall[m][pl.ds(e * 4, 4)].reshape(512, 256).astype(jnp.float32)
        elif kind == 3:
            total = component(n // 4, n % 4, total)
        elif kind == 1:
            copies[NAMES[n]].wait_recv()
        elif NAMES[n][0] in "UV":
            residual(NAMES[n])
        else:
            panel(NAMES[n])

    mine = total * -cond_ref[...]
    weighted = mine[0:1] * gw_ref[0]
    for t in range(1, 8):
        weighted = weighted + mine[t : t + 1] * gw_ref[t]
    part[...] = mine
    row[...] = weighted
    for n, device in enumerate(peers):
        go(f"G{n}", part, gath.at[e], device)
    for n, device in enumerate(peers):
        go(f"H{n}", row, rows.at[g, e], device)
    for n, device in enumerate(cross):
        go(f"I{n}", row, rows.at[g, e], device)
    gath[e] = mine
    rows[g, e] = weighted
    for name in copies:
        if name[0] not in "GHI":
            copies[name].wait_send()
    for name in copies:
        if name[0] in "GHI":
            copies[name].wait_recv()
    grad_ref[...] = (gath[0] + gath[1]) + (gath[2] + gath[3])
    each = [(rows[n, 0] + rows[n, 1]) + (rows[n, 2] + rows[n, 3]) for n in range(2)]
    upd_ref[...] = each[0] + each[1]
    for name in copies:
        if name[0] in "GHI":
            copies[name].wait_send()


def per_device(panels, conductivity, residuals, gate_weight, pattern, live_count):
    vmem = pl.BlockSpec(memory_space=pltpu.VMEM)
    hbm = pl.BlockSpec(memory_space=pl.ANY)
    copies = 128
    grad, update = pl.pallas_call(
        kernel,
        out_shape=(
            pltpu.VMEM((8, 256), jnp.float32),
            pltpu.VMEM((1, 256), jnp.float32),
        ),
        in_specs=[hbm] * 6,
        out_specs=(vmem, vmem),
        scratch_shapes=[
            pltpu.VMEM((1, 256), jnp.float32),
            pltpu.SMEM((8,), jnp.float32),
            pltpu.SMEM((4, 4), jnp.int32),
            pltpu.SMEM((4,), jnp.int32),
            pltpu.VMEM((32, 16, 32, 128), jnp.bfloat16),
            pltpu.VMEM((16, 128, 256), jnp.bfloat16),
            pltpu.VMEM((16, 128, 256), jnp.bfloat16),
            pltpu.VMEM((16, 128, 256), jnp.bfloat16),
            pltpu.VMEM((3, 3, 2, 128, 256), jnp.bfloat16),
            pltpu.VMEM((3, 512, 256), jnp.float32),
            pltpu.VMEM((512, 128), jnp.bfloat16),
            pltpu.VMEM((256, 256), jnp.float32),
            pltpu.VMEM((8, 256), jnp.float32),
            pltpu.VMEM((1, 256), jnp.float32),
            pltpu.VMEM((4, 8, 256), jnp.float32),
            pltpu.VMEM((2, 4, 1, 256), jnp.float32),
            pltpu.SemaphoreType.DMA((copies,)),
            pltpu.SemaphoreType.DMA((copies,)),
            pltpu.SemaphoreType.DMA((8,)),
        ],
        compiler_params=pltpu.CompilerParams(
            collective_id=0, has_side_effects=True, vmem_limit_bytes=60 << 20
        ),
        name="adjoint",
    )(
        panels.reshape(3, 4, 128, 256),
        residuals.reshape(512, 128),
        conductivity.reshape(1, 256),
        gate_weight,
        pattern,
        live_count,
    )
    return grad, update.reshape(256)


def solution(mesh):
    return jax.shard_map(
        per_device,
        mesh=mesh,
        in_specs=(
            P(None, "elec", "cell"),
            P("cell"),
            P("gate", "elec", None, "cell", None),
            P("gate"),
            P("elec", None),
            P("elec"),
        ),
        out_specs=(P("gate", "cell"), P("cell")),
        check_vma=False,
    )
```
